32 devices in a mesh: ax: 4 (over y, x), az: 8 (over z, core).
Axes of the slice: x: 2, y: 2, z: 4, core: 2. Of those that a mesh axis runs over, the one named last changes fastest.
Arguments:
- saved_flow: float32 [3, 256, 64, 1024], P(None, 'az', None, 'ax'), may hold values from -6 to 6
- saved_adjoint: float32 [3, 256, 64, 1024], P(None, 'az', None, 'ax'), may hold values from -6 to 6
- tangent: float32 [3, 256, 64, 1024], P(None, 'az', None, 'ax'), may hold values from -6 to 6
- second_adjoint: float32 [3, 256, 64, 1024], P(None, 'az', None, 'ax'), may hold values from -6 to 6
- radial_rate: float32 [64], replicated, may hold values from 1 to 100
Outputs:
- tangent_next: float32 [3, 256, 64, 1024], P(None, 'az', None, 'ax')
- second_next: float32 [3, 256, 64, 1024], P(None, 'az', None, 'ax')
The draws below stay inside these ranges and needn't reach their ends.
All inputs are finite; a program needn't handle non-finite values.
Results may differ from the reference program's by a relative error of at most 0.00005.
Values sent between devices are 32-bit elements; how exact they have to be, the bound alone decides.
A program may use at most 192 MiB of HBM per device.

```python
import math
import jax
import jax.numpy as jnp
from jax import lax

NR = 64
MA = 256
KX = 1024


def block_scale(stream_key, dims, cuts, least, largest):
    loudness, own = 1.0, jax.random.fold_in(stream_key, 6)
    for axis_at, blocks in cuts:
        steps = jnp.exp(jax.random.uniform(jax.random.fold_in(own, axis_at), (blocks,), jnp.float32, least / len(cuts), largest / len(cuts)))
        loudness = loudness * jnp.repeat(steps, dims[axis_at] // blocks).reshape([-1 if axis == axis_at else 1 for axis in range(len(dims))])
    return loudness


def bell_draw(rng, extent, width, most, cuts=(), kind=jnp.bfloat16):
    array = width * jax.random.normal(rng, extent, jnp.float32)
    if cuts:
        array = array * block_scale(rng, extent, cuts, -0.22, 0.18)
    return jnp.clip(array, -most, most).astype(kind)


def setup_inputs(seed: int = 0) -> dict:
    keys = jax.random.split(jax.random.key(seed), 6)
    saved_flow = bell_draw(keys[0], (3, MA, NR, KX), 1.0, 6.0, ((1, 8), (3, 4)), jnp.float32)
    saved_adjoint = bell_draw(keys[1], (3, MA, NR, KX), 1.0, 6.0, ((1, 8), (3, 4)), jnp.float32)
    tangent = bell_draw(keys[2], (3, MA, NR, KX), 1.0, 6.0, ((1, 8), (3, 4)), jnp.float32)
    second_adjoint = bell_draw(keys[3], (3, MA, NR, KX), 1.0, 6.0, ((1, 8), (3, 4)), jnp.float32)
    radial_rate = jnp.clip(jnp.exp(jax.random.uniform(keys[4], (NR,), jnp.float32, math.log(1.0), math.log(100.0))), 1.0, 100.0)
    return dict(saved_flow=saved_flow, saved_adjoint=saved_adjoint, tangent=tangent, second_adjoint=second_adjoint, radial_rate=radial_rate)


time_step = 0.1
viscosity = 0.005
axial_unit = 2.0 * math.pi / 20.0

def radial_table(count):
    points = jnp.arange(count, dtype=jnp.int32)[:, None]
    orders = jnp.arange(count, dtype=jnp.int32)[None, :]
    phases = orders * (2 * points + 1) % (4 * count)
    values = jnp.cos(phases.astype(jnp.float32) * (math.pi / (2.0 * count)))
    scales = jnp.where(orders == 0, math.sqrt(1.0 / count), math.sqrt(2.0 / count))
    return (values * scales).astype(jnp.float32)

def hartley(field, axis):
    length = field.shape[axis]
    spectrum = jnp.fft.fft(field, axis=axis)
    return (spectrum.real - spectrum.imag) / math.sqrt(length)

def to_physical(field, table):
    grid = jnp.einsum('jr,cmrk->cmjk', table, field, precision=lax.Precision.HIGHEST)
    return hartley(hartley(grid, 1), 3)

def to_spectral(field, table):
    spectral = hartley(hartley(field, 3), 1)
    return jnp.einsum('jr,cmjk->cmrk', table, spectral, precision=lax.Precision.HIGHEST)

def damping(radial_rate):
    azimuth = jnp.arange(MA, dtype=jnp.int32)
    wave_azimuth = jnp.minimum(azimuth, MA - azimuth).astype(jnp.float32)
    axial = jnp.arange(KX, dtype=jnp.int32)
    wave_axial = jnp.minimum(axial, KX - axial).astype(jnp.float32) * axial_unit
    total = radial_rate[None, :, None] + (wave_azimuth ** 2)[:, None, None] + (wave_axial ** 2)[None, None, :]
    return 1.0 + viscosity * total

def reference(saved_flow, saved_adjoint, tangent, second_adjoint, radial_rate):
    table = radial_table(NR)
    flow = to_physical(saved_flow, table)
    adjoint = to_physical(saved_adjoint, table)
    tang = to_physical(tangent, table)
    second = to_physical(second_adjoint, table)
    flow_sum = lax.optimization_barrier(jnp.sum(flow, axis=0))[None]
    adjoint_sum = lax.optimization_barrier(jnp.sum(adjoint, axis=0))[None]
    tang_sum = lax.optimization_barrier(jnp.sum(tang, axis=0))[None]
    second_sum = lax.optimization_barrier(jnp.sum(second, axis=0))[None]
    tangent_rhs = flow * tang_sum + tang * flow_sum
    second_rhs = flow * second_sum + second * flow_sum + adjoint * tang_sum + tang * adjoint_sum
    tangent_term = to_spectral(tangent_rhs, table)
    second_term = to_spectral(second_rhs, table)
    denom = damping(radial_rate)[None]
    tangent_next = (tangent + time_step * tangent_term) / denom
    second_next = (second_adjoint + time_step * second_term) / denom
    return (tangent_next, second_next)
```

```python
import functools
import math

import jax
import jax.numpy as jnp
import ml_dtypes
import numpy as np
from jax import lax
from jax.experimental import pallas as pl
from jax.experimental.pallas import tpu as pltpu
from jax.sharding import PartitionSpec as P

time_step = 0.1
viscosity = 0.005
axial_unit = 2.0 * math.pi / 20.0
lookahead = 3
MESH = pl.DeviceIdType.MESH


def radial_table(count):
    points = np.arange(count)[:, None]
    orders = np.arange(count)[None, :]
    phases = orders * (2 * points + 1) % (4 * count)
    values = np.cos(phases * (math.pi / (2.0 * count)))
    scales = np.where(orders == 0, math.sqrt(1.0 / count), math.sqrt(2.0 / count))
    return values * scales


def hartley_table(length):
    phases = np.arange(length)[:, None] * np.arange(length)[None, :] % length
    angles = phases * (2.0 * math.pi / length)
    return (np.cos(angles) + np.sin(angles)) / math.sqrt(length)


def halves(table):
    high = table.astype(ml_dtypes.bfloat16)
    low = (table - high.astype(np.float64)).astype(ml_dtypes.bfloat16)
    return jnp.asarray(np.stack((high, low)))


def split(value):
    high = value.astype(jnp.bfloat16)
    low = (value - high.astype(jnp.float32)).astype(jnp.bfloat16)
    return high, low


def dot(left, right):
    return jnp.dot(left, right, preferred_element_type=jnp.float32)


def kernel(
    az,
    ax,
    grid_ref,
    azimuth_ref,
    axial_ref,
    out_ref,
    back_ref,
    columns,
    rows,
    high_rows,
    low_rows,
    send_in,
    recv_in,
    send_over,
    recv_over,
    send_back,
    recv_back,
    send_out,
    recv_out,
    own,
):
    steps, fields, azimuth_count, local_axial = columns.shape
    produced = out_ref.shape[1]
    local_azimuth = azimuth_count // az
    middle = azimuth_count // ax
    axial_count = rows.shape[3]
    group = high_rows.shape[0] // middle
    my_az = lax.axis_index("az")
    my_ax = lax.axis_index("ax")

    def az_rows(place):
        return pl.ds(pl.multiple_of(place * local_azimuth, local_azimuth), local_azimuth)

    def ax_rows(place):
        return pl.ds(pl.multiple_of(place * middle, middle), middle)

    def ax_lanes(place):
        return pl.ds(pl.multiple_of(place * local_axial, local_axial), local_axial)

    def copy_in(step, hop):
        target = (my_az + hop) % az
        return pltpu.make_async_remote_copy(
            src_ref=grid_ref.at[target * steps + step],
            dst_ref=columns.at[step, :, az_rows(my_az), :],
            send_sem=send_in.at[step, hop - 1],
            recv_sem=recv_in.at[step, hop - 1],
            device_id={"az": target},
            device_id_type=MESH,
        )

    def own_in(step):
        return pltpu.make_async_copy(
            grid_ref.at[my_az * steps + step],
            columns.at[step, :, az_rows(my_az), :],
            own.at[0, step],
        )

    def copy_over(step, hop):
        target = (my_ax + hop) % ax
        return pltpu.make_async_remote_copy(
            src_ref=columns.at[step, :, ax_rows(target), :],
            dst_ref=rows.at[step, :, :, ax_lanes(my_ax)],
            send_sem=send_over.at[step, hop - 1],
            recv_sem=recv_over.at[step, hop - 1],
            device_id={"ax": target},
            device_id_type=MESH,
        )

    def own_over(step):
        return pltpu.make_async_copy(
            columns.at[step, :, ax_rows(my_ax), :],
            rows.at[step, :, :, ax_lanes(my_ax)],
            own.at[1, step],
        )

    def copy_back(step, hop):
        target = (my_ax + hop) % ax
        return pltpu.make_async_remote_copy(
            src_ref=rows.at[step, pl.ds(0, produced), :, ax_lanes(target)],
            dst_ref=back_ref.at[step, :, ax_rows(my_ax), :],
            send_sem=send_back.at[step, hop - 1],
            recv_sem=recv_back.at[step, hop - 1],
            device_id={"ax": target},
            device_id_type=MESH,
        )

    def own_back(step):
        return pltpu.make_async_copy(
            rows.at[step, pl.ds(0, produced), :, ax_lanes(my_ax)],
            back_ref.at[step, :, ax_rows(my_ax), :],
            own.at[2, step],
        )

    def copy_out(step, hop):
        target = (my_az + hop) % az
        return pltpu.make_async_remote_copy(
            src_ref=columns.at[step, pl.ds(0, produced), az_rows(target), :],
            dst_ref=out_ref.at[my_az * steps + step],
            send_sem=send_out.at[step, hop - 1],
            recv_sem=recv_out.at[step, hop - 1],
            device_id={"az": target},
            device_id_type=MESH,
        )

    def own_out(step):
        return pltpu.make_async_copy(
            columns.at[step, pl.ds(0, produced), az_rows(my_az), :],
            out_ref.at[my_az * steps + step],
            own.at[3, step],
        )

    def start(count, copy, mine, step):
        def each(hop, carry):
            copy(step, hop).start()
            return carry

        lax.fori_loop(1, count, each, 0)
        mine(step).start()

    def arrive(count, copy, mine, step):
        def each(hop, carry):
            copy(step, hop).wait_recv()
            return carry

        mine(step).wait()
        lax.fori_loop(1, count, each, 0)

    def leave(count, copy, step):
        def each(hop, carry):
            copy(step, hop).wait_send()
            return carry

        lax.fori_loop(1, count, each, 0)

    def along_azimuth(step, count):
        def each(field, carry):
            high, low = split(columns[step, field])
            columns[step, field] = dot(azimuth_ref[0], high) + (
                dot(azimuth_ref[1], high) + dot(azimuth_ref[0], low)
            )
            return carry

        lax.fori_loop(0, count, each, 0)

    tile = min(256, axial_count)

    def along_axial(step, count):
        def each(part, carry):
            first = part * group

            def cast(place, carry):
                high, low = split(rows[step, first + place])
                at = pl.ds(pl.multiple_of(place * middle, middle), middle)
                high_rows[at, :] = high
                low_rows[at, :] = low
                return carry

            lax.fori_loop(0, group, cast, 0)

            def turn(place, carry):
                lanes = pl.ds(pl.multiple_of(place * tile, tile), tile)
                high = axial_ref[0, :, lanes]
                low = axial_ref[1, :, lanes]
                value = dot(high_rows[...], high) + (
                    dot(high_rows[...], low) + dot(low_rows[...], high)
                )
                rows[step, pl.ds(first, group), :, lanes] = value.reshape(group, middle, tile)
                return carry

            lax.fori_loop(0, axial_count // tile, turn, 0)
            return carry

        lax.fori_loop(0, count // group, each, 0)

    def multiply(step):
        components = fields // 4

        def each(place, carry):
            at = pl.ds(pl.multiple_of(place * 8, 8), 8)
            for first in range(0, axial_count, tile):
                lanes = pl.ds(first, tile)
                values = [rows[step, field, at, lanes] for field in range(fields)]
                flow = values[0:components]
                adjoint = values[components : 2 * components]
                tang = values[2 * components : 3 * components]
                second = values[3 * components : 4 * components]
                flow_sum, adjoint_sum, tang_sum, second_sum = (
                    functools.reduce(lambda a, b: a + b, part)
                    for part in (flow, adjoint, tang, second)
                )
                for c in range(components):
                    rows[step, c, at, lanes] = flow[c] * tang_sum + tang[c] * flow_sum
                    rows[step, components + c, at, lanes] = (
                        flow[c] * second_sum
                        + second[c] * flow_sum
                        + adjoint[c] * tang_sum
                        + tang[c] * adjoint_sum
                    )
            return carry

        lax.fori_loop(0, middle // 8, each, 0)

    barrier = pltpu.get_barrier_semaphore()

    def greet_az(hop, carry):
        pl.semaphore_signal(
            barrier, inc=1, device_id={"az": (my_az + hop) % az}, device_id_type=MESH
        )
        return carry

    def greet_ax(hop, carry):
        pl.semaphore_signal(
            barrier, inc=1, device_id={"ax": (my_ax + hop) % ax}, device_id_type=MESH
        )
        return carry

    lax.fori_loop(1, az, greet_az, 0)
    lax.fori_loop(1, ax, greet_ax, 0)
    pl.semaphore_wait(barrier, az + ax - 2)

    for step in range(min(lookahead, steps)):
        start(az, copy_in, own_in, step)

    def turn(now, carry):
        @pl.when(now < steps)
        def _():
            arrive(az, copy_in, own_in, now)

            @pl.when(now + lookahead < steps)
            def _():
                start(az, copy_in, own_in, now + lookahead)

            along_azimuth(now, fields)
            start(ax, copy_over, own_over, now)

        @pl.when((now >= 1) & (now < steps + 1))
        def _():
            step = now - 1
            arrive(ax, copy_over, own_over, step)
            along_axial(step, fields)
            multiply(step)
            along_axial(step, produced)
            start(ax, copy_back, own_back, step)

        @pl.when(now >= 2)
        def _():
            step = now - 2
            leave(ax, copy_over, step)
            arrive(ax, copy_back, own_back, step)
            fetch = pltpu.make_async_copy(
                back_ref.at[step], columns.at[step, pl.ds(0, produced)], own.at[4, step]
            )
            fetch.start()
            fetch.wait()
            along_azimuth(step, produced)
            start(az, copy_out, own_out, step)

        return carry

    lax.fori_loop(0, steps + 2, turn, 0)

    def finish(step, carry):
        arrive(az, copy_out, own_out, step)
        leave(az, copy_in, step)
        leave(ax, copy_back, step)
        leave(az, copy_out, step)
        return carry

    lax.fori_loop(0, steps, finish, 0)


def exchange(grid, az, ax):
    radial_count, fields, local_azimuth, local_axial = grid.shape
    azimuth_count = local_azimuth * az
    axial_count = local_axial * ax
    steps = radial_count // az
    produced = fields // 2
    middle = azimuth_count // ax
    columns = (steps, fields, azimuth_count, local_axial)
    rows = (steps, fields, middle, axial_count)
    group_rows = produced * middle
    points = radial_count * fields * azimuth_count * axial_count // (az * ax)
    semaphores = lambda count: pltpu.SemaphoreType.DMA((steps, count - 1))
    return pl.pallas_call(
        functools.partial(kernel, az, ax),
        out_shape=[
            jax.ShapeDtypeStruct(
                (radial_count, produced, local_azimuth, local_axial), jnp.float32
            ),
            jax.ShapeDtypeStruct((steps, produced, azimuth_count, local_axial), jnp.float32),
        ],
        in_specs=[
            pl.BlockSpec(memory_space=pl.ANY),
            pl.BlockSpec(memory_space=pltpu.VMEM),
            pl.BlockSpec(memory_space=pltpu.VMEM),
        ],
        out_specs=[pl.BlockSpec(memory_space=pl.ANY)] * 2,
        scratch_shapes=[
            pltpu.VMEM(columns, jnp.float32),
            pltpu.VMEM(rows, jnp.float32),
            pltpu.VMEM((group_rows, axial_count), jnp.bfloat16),
            pltpu.VMEM((group_rows, axial_count), jnp.bfloat16),
            semaphores(az),
            semaphores(az),
            semaphores(ax),
            semaphores(ax),
            semaphores(ax),
            semaphores(ax),
            semaphores(az),
            semaphores(az),
            pltpu.SemaphoreType.DMA((5, steps)),
        ],
        compiler_params=pltpu.CompilerParams(
            collective_id=0, has_side_effects=True, vmem_limit_bytes=60 * 2**20
        ),
        cost_estimate=pl.CostEstimate(
            flops=9 * points * (azimuth_count + axial_count),
            bytes_accessed=8 * points,
            transcendentals=0,
        ),
        name="exchange",
    )(grid, halves(hartley_table(azimuth_count)), halves(hartley_table(axial_count)))[0]


def dot_split(table_ref, value):
    high, low = split(value)
    return dot(table_ref[0], high) + (dot(table_ref[1], high) + dot(table_ref[0], low))


def to_grid_kernel(table_ref, flow_ref, adjoint_ref, tangent_ref, second_ref, out_ref):
    _, rows, radial_count, lanes = flow_ref.shape
    for field, ref in enumerate((flow_ref, adjoint_ref, tangent_ref, second_ref)):
        value = dot_split(table_ref, ref[0].reshape(rows * radial_count, lanes))
        out_ref[:, field, 0] = value.reshape(radial_count, rows, lanes)


def to_grid(table, fields):
    components, local_azimuth, radial_count, local_axial = fields[0].shape
    count = len(fields)
    out = pl.pallas_call(
        to_grid_kernel,
        grid=(local_azimuth // 8, components),
        out_shape=jax.ShapeDtypeStruct(
            (radial_count, count, components, local_azimuth, local_axial), jnp.float32
        ),
        in_specs=[pl.BlockSpec(table.shape, lambda m, c: (0, 0, 0))]
        + [pl.BlockSpec((1, 8, radial_count, local_axial), lambda m, c: (c, m, 0, 0))] * count,
        out_specs=pl.BlockSpec(
            (radial_count, count, 1, 8, local_axial), lambda m, c: (0, 0, c, m, 0)
        ),
        compiler_params=pltpu.CompilerParams(vmem_limit_bytes=40 * 2**20),
        name="to_grid",
    )(table, *fields)
    return out.reshape(radial_count, count * components, local_azimuth, local_axial)


def from_grid_kernel(
    table_ref, turned_ref, tangent_ref, second_ref, rate_ref, axial_ref, next_ref, after_ref
):
    _, rows, radial_count, lanes = tangent_ref.shape
    denom = 1.0 + viscosity * (rate_ref[...] + axial_ref[...].reshape(1, 1, lanes))
    for field, (ref, out_ref) in enumerate(((tangent_ref, next_ref), (second_ref, after_ref))):
        value = turned_ref[:, field, 0].reshape(radial_count * rows, lanes)
        term = dot_split(table_ref, value).reshape(rows, radial_count, lanes)
        out_ref[0] = (ref[0] + time_step * term) / denom


def from_grid(table, turned, tangent, second_adjoint, rate, axial):
    components, local_azimuth, radial_count, local_axial = tangent.shape
    turned = turned.reshape(radial_count, 2, components, local_azimuth, local_axial)
    spectral = pl.BlockSpec((1, 8, radial_count, local_axial), lambda m, c: (c, m, 0, 0))
    return pl.pallas_call(
        from_grid_kernel,
        grid=(local_azimuth // 8, components),
        out_shape=[jax.ShapeDtypeStruct(tangent.shape, jnp.float32)] * 2,
        in_specs=[
            pl.BlockSpec(table.shape, lambda m, c: (0, 0, 0)),
            pl.BlockSpec((radial_count, 2, 1, 8, local_axial), lambda m, c: (0, 0, c, m, 0)),
            spectral,
            spectral,
            pl.BlockSpec((8, radial_count, 1), lambda m, c: (m, 0, 0)),
            pl.BlockSpec((1, local_axial), lambda m, c: (0, 0)),
        ],
        out_specs=[spectral] * 2,
        compiler_params=pltpu.CompilerParams(vmem_limit_bytes=40 * 2**20),
        name="from_grid",
    )(table, turned, tangent, second_adjoint, rate, axial)


def body(saved_flow, saved_adjoint, tangent, second_adjoint, radial_rate):
    local_azimuth = tangent.shape[1]
    radial_count = tangent.shape[2]
    local_axial = tangent.shape[3]
    az = lax.axis_size("az")
    ax = lax.axis_size("ax")
    azimuth_count = local_azimuth * az
    axial_count = local_axial * ax
    table = np.einsum("jr,mn->jmnr", radial_table(radial_count), np.eye(8))
    table = table.reshape(8 * radial_count, 8 * radial_count)
    grid = to_grid(halves(table), (saved_flow, saved_adjoint, tangent, second_adjoint))
    turned = exchange(grid, az, ax)
    azimuth = lax.axis_index("az") * local_azimuth + jnp.arange(local_azimuth, dtype=jnp.int32)
    wave_azimuth = jnp.minimum(azimuth, azimuth_count - azimuth).astype(jnp.float32)
    axial = lax.axis_index("ax") * local_axial + jnp.arange(local_axial, dtype=jnp.int32)
    wave_axial = jnp.minimum(axial, axial_count - axial).astype(jnp.float32) * axial_unit
    rate = radial_rate[None, :, None] + (wave_azimuth**2)[:, None, None]
    return tuple(
        from_grid(
            halves(table.T), turned, tangent, second_adjoint, rate, (wave_axial**2)[None, :]
        )
    )


def solution(mesh):
    in_specs = (
        P(None, "az", None, "ax"),
        P(None, "az", None, "ax"),
        P(None, "az", None, "ax"),
        P(None, "az", None, "ax"),
        P(),
    )
    out_specs = (P(None, "az", None, "ax"), P(None, "az", None, "ax"))
    return jax.shard_map(body, mesh=mesh, in_specs=in_specs, out_specs=out_specs, check_vma=False)
```
